256 devices in a mesh: space: 16 (over z_hi, x, core), tm: 16 (over z_lo, y).
Axes of the slice: x: 4, y: 4, z: 8 (z_hi: 2, z_lo: 4; z = z_hi * 4 + z_lo), core: 2. Of those that a mesh axis runs over, the one named last changes fastest.
Arguments:
- query_space: bfloat16 [2, 16, 1024, 2048], P(None, 'tm', 'space'), may hold values from -10 to 10
- key_space: bfloat16 [2, 16, 1024, 2048], P(None, 'tm', 'space'), may hold values from -10 to 10
- value_space: bfloat16 [2, 16, 1024, 2048], P(None, 'tm', 'space'), may hold values from -6 to 6
- query_time: bfloat16 [2, 16, 1024, 2048], P(None, 'tm', 'space'), may hold values from -10 to 10
- key_time: bfloat16 [2, 16, 1024, 2048], P(None, 'tm', 'space'), may hold values from -10 to 10
- value_time: bfloat16 [2, 16, 1024, 2048], P(None, 'tm', 'space'), may hold values from -6 to 6
- block_grad: bfloat16 [2, 16, 1024, 2048], P(None, 'tm', 'space'), may hold values from -6 to 6
- branch_grad: bfloat16 [2, 16, 1024, 2048], P(None, 'tm', 'space'), may hold values from -6 to 6
- proj_space: bfloat16 [2048, 2048], P('space'), may hold values from -0.5 to 0.5
- proj_time: bfloat16 [2048, 2048], P('tm'), may hold values from -0.5 to 0.5
Outputs:
- grad_query_space: bfloat16 [2, 16, 1024, 2048], P(None, 'tm', 'space')
- grad_key_space: bfloat16 [2, 16, 1024, 2048], P(None, 'tm', 'space')
- grad_value_space: bfloat16 [2, 16, 1024, 2048], P(None, 'tm', 'space')
- grad_query_time: bfloat16 [2, 16, 1024, 2048], P(None, 'tm', 'space')
- grad_key_time: bfloat16 [2, 16, 1024, 2048], P(None, 'tm', 'space')
- grad_value_time: bfloat16 [2, 16, 1024, 2048], P(None, 'tm', 'space')
The draws below stay inside these ranges and needn't reach their ends.
All inputs are finite; a program needn't handle non-finite values.
Results may differ from the reference program's by a relative error of at most 0.011.
Values may be sent and summed in bfloat16 or wider, within the bound.
No kernel may reach another device: no remote copies, remote signals or barrier semaphores. Data moves between devices by JAX's collectives and lax.ppermute only.
A program may use at most 128 MiB of HBM per device.

```python
import math
import jax
import jax.numpy as jnp
from jax import lax

DM = 2048
HEADS = 16
HEAD_DIM = 128
DW = 2048
B = 2
P_SIZE = 1024
FRAMES = 16


def draw_query_space(key, part):
    key = jax.random.fold_in(key, 11)
    sample_field = jnp.clip(jax.random.normal(key, (B, FRAMES, P_SIZE, DW), jnp.float32), -6.0, 6.0)
    return sample_field.astype(jnp.bfloat16)


def draw_key_space(key, part):
    key = jax.random.fold_in(key, 12)
    sample_field = jnp.clip(jax.random.normal(key, (B, FRAMES, P_SIZE, DW), jnp.float32), -6.0, 6.0)
    return sample_field.astype(jnp.bfloat16)


def draw_query_time(key, part):
    key = jax.random.fold_in(key, 13)
    sample_field = jnp.clip(jax.random.normal(key, (B, FRAMES, P_SIZE, DW), jnp.float32), -6.0, 6.0)
    return sample_field.astype(jnp.bfloat16)


def draw_key_time(key, part):
    key = jax.random.fold_in(key, 14)
    sample_field = jnp.clip(jax.random.normal(key, (B, FRAMES, P_SIZE, DW), jnp.float32), -6.0, 6.0)
    return sample_field.astype(jnp.bfloat16)


def steps_of(key, shape, cuts, smallest, high):
    level = 1.0
    for position, parts in cuts:
        steps = jax.random.uniform(jax.random.fold_in(jax.random.fold_in(key, 6), position), (parts,), jnp.float32, smallest / len(cuts), high / len(cuts))
        level = level * jnp.repeat(jnp.exp(steps), shape[position] // parts).reshape((-1,) + (1,) * (len(shape) - 1 - position))
    return level


def normal_values(rng, extent, deviation, limit, shards=(), held_as=jnp.bfloat16):
    result = deviation * jax.random.normal(rng, extent, jnp.float32)
    if shards:
        result = result * steps_of(rng, extent, shards, -0.22, 0.18)
    return jnp.clip(result, -limit, limit).astype(held_as)


def setup_inputs(seed: int = 0) -> dict:
    streams_of = jax.random.split(jax.random.key(seed), 11)
    query_space = draw_query_space(jax.random.fold_in(streams_of[10], 71), 0)
    key_space = draw_key_space(jax.random.fold_in(streams_of[10], 71), 0)
    value_space = normal_values(streams_of[2], (B, FRAMES, P_SIZE, DW), 1.0, 6.0, ((1, 16), (2, 16)))
    query_time = draw_query_time(jax.random.fold_in(streams_of[10], 71), 0)
    key_time = draw_key_time(jax.random.fold_in(streams_of[10], 71), 0)
    value_time = normal_values(streams_of[5], (B, FRAMES, P_SIZE, DW), 1.0, 6.0, ((1, 16), (2, 16)))
    block_grad = normal_values(streams_of[6], (B, FRAMES, P_SIZE, DM), 1.0, 6.0, ((1, 16), (2, 16)))
    branch_grad = normal_values(streams_of[7], (B, FRAMES, P_SIZE, DM), 1.0, 6.0, ((1, 16), (2, 16)))
    proj_space = normal_values(streams_of[8], (DW, DM), (DM // 16) ** -0.5, 0.5, ((0, 16),))
    proj_time = normal_values(streams_of[9], (DW, DM), (DM // 16) ** -0.5, 0.5, ((0, 16),))
    return dict(query_space=query_space, key_space=key_space, value_space=value_space, query_time=query_time, key_time=key_time, value_time=value_time, block_grad=block_grad, branch_grad=branch_grad, proj_space=proj_space, proj_time=proj_time)


def head_backward(query_matrix, key_matrix, value_matrix, output_matrix):
    logit_scale = 1.0 / math.sqrt(HEAD_DIM)
    attention_logits = jnp.einsum('ogn,ofn->ogf', query_matrix.astype(jnp.float32), key_matrix.astype(jnp.float32)) * logit_scale
    row_top = lax.optimization_barrier(jnp.max(attention_logits, axis=-1, keepdims=True))
    expo_terms = jnp.exp(attention_logits - row_top)
    probabilities = expo_terms / lax.optimization_barrier(jnp.sum(expo_terms, axis=-1, keepdims=True))
    attention_weights = probabilities.astype(jnp.bfloat16)
    value_gradient = jnp.einsum('gfp,gfq->gpq', attention_weights.astype(jnp.float32), output_matrix.astype(jnp.float32)).astype(jnp.bfloat16)
    probability_gradient = jnp.einsum('ogn,ofn->ogf', output_matrix.astype(jnp.float32), value_matrix.astype(jnp.float32))
    row_delta = lax.optimization_barrier(jnp.sum(probabilities * probability_gradient, axis=-1, keepdims=True))
    score_gradient = (probabilities * (probability_gradient - row_delta)).astype(jnp.bfloat16)
    query_gradient = (jnp.einsum('wfc,wci->wfi', score_gradient.astype(jnp.float32), key_matrix.astype(jnp.float32)) * logit_scale).astype(jnp.bfloat16)
    key_gradient = (jnp.einsum('gfp,gfq->gpq', score_gradient.astype(jnp.float32), query_matrix.astype(jnp.float32)) * logit_scale).astype(jnp.bfloat16)
    return (query_gradient, key_gradient, value_gradient)

def split_heads(array_in):
    seqs, length, width = array_in.shape
    return array_in.reshape(seqs, length, HEADS, HEAD_DIM).transpose(2, 0, 1, 3)

def join_heads(array_in):
    count, seqs, length, depth = array_in.shape
    return array_in.transpose(1, 2, 0, 3).reshape(seqs, length, count * depth)

def all_heads(query_matrix, key_matrix, value_matrix, output_matrix):
    grouped = (split_heads(query_matrix), split_heads(key_matrix), split_heads(value_matrix), split_heads(output_matrix))
    results = lax.map(lambda group: head_backward(group[0], group[1], group[2], group[3]), grouped)
    return tuple((join_heads(result_part) for result_part in results))

def frames_first(array_in):
    return array_in.reshape(B * FRAMES, P_SIZE, array_in.shape[-1])

def frames_back(array_in):
    return array_in.reshape(B, FRAMES, P_SIZE, array_in.shape[-1])

def lines_first(array_in):
    return array_in.transpose(0, 2, 1, 3).reshape(B * P_SIZE, FRAMES, array_in.shape[-1])

def lines_back(array_in):
    return array_in.reshape(B, P_SIZE, FRAMES, array_in.shape[-1]).transpose(0, 2, 1, 3)

def reference(query_space, key_space, value_space, query_time, key_time, value_time, block_grad, branch_grad, proj_space, proj_time):
    space_out = jnp.dot(block_grad.reshape(-1, DM), proj_space.T, preferred_element_type=jnp.float32).astype(jnp.bfloat16)
    space_out = space_out.reshape(B, FRAMES, P_SIZE, DW)
    space_grads = all_heads(frames_first(query_space), frames_first(key_space), frames_first(value_space), frames_first(space_out))
    time_cotangent = (block_grad.astype(jnp.float32) + branch_grad.astype(jnp.float32)).astype(jnp.bfloat16)
    time_out = jnp.dot(time_cotangent.reshape(-1, DM), proj_time.T, preferred_element_type=jnp.float32).astype(jnp.bfloat16)
    time_out = time_out.reshape(B, FRAMES, P_SIZE, DW)
    time_grads = all_heads(lines_first(query_time), lines_first(key_time), lines_first(value_time), lines_first(time_out))
    return (frames_back(space_grads[0]), frames_back(space_grads[1]), frames_back(space_grads[2]), lines_back(time_grads[0]), lines_back(time_grads[1]), lines_back(time_grads[2]))
```

```python
import functools
import math

import jax
import jax.numpy as jnp
from jax import lax
from jax.experimental import pallas as pl
from jax.experimental.pallas import tpu as pltpu
from jax.sharding import PartitionSpec as P

HEAD_DIM = 128
SCALE = 1.0 / math.sqrt(HEAD_DIM)
LOG2E = math.log2(math.e)
VMEM = 48 * 1024 * 1024
BF16 = jnp.bfloat16
F32 = jnp.float32


def permutation(move):
    pairs = []
    for s in range(16):
        for t in range(16):
            z, x, y, c = (s // 8) * 4 + t // 4, (s // 2) % 4, t % 4, s % 2
            z2, x2, y2, c2 = move(z, x, y, c)
            z2, x2, y2, c2 = z2 % 8, x2 % 4, y2 % 4, c2 % 2
            pairs.append((s * 16 + t, ((z2 // 4) * 8 + x2 * 2 + c2) * 16 + (z2 % 4) * 4 + y2))
    return pairs


def send(array, move):
    return lax.ppermute(array, ("space", "tm"), permutation(move))


def nt(a, b):
    return lax.dot_general(a, b, (((1,), (1,)), ((), ())), preferred_element_type=F32)


def nn(a, b):
    return lax.dot_general(a, b, (((1,), (0,)), ((), ())), preferred_element_type=F32)


def call(kernel, out_shape, flops, size, **kw):
    return pl.pallas_call(
        kernel,
        out_shape=out_shape,
        compiler_params=pltpu.CompilerParams(vmem_limit_bytes=VMEM),
        cost_estimate=pl.CostEstimate(flops=flops, bytes_accessed=size, transcendentals=0),
        **kw,
    )


def pack_kernel(a_ref, b_ref, c_ref, out_ref):
    for t, ref in enumerate((a_ref, b_ref, c_ref)):
        for h in range(16):
            out_ref[h, t] = ref[:, h * 128 : (h + 1) * 128]


def pack(a, b, c):
    flat = [v.reshape(128, 2048) for v in (a, b, c)]
    out = call(pack_kernel, jax.ShapeDtypeStruct((16, 3, 128, 128), BF16), 0, 3 << 20)(*flat)
    return out.reshape(16, 3, 2, 64, 128)


def unpack_kernel(in_ref, a_ref, b_ref, c_ref):
    for t, ref in enumerate((a_ref, b_ref, c_ref)):
        for h in range(16):
            ref[:, h * 128 : (h + 1) * 128] = in_ref[h, t]


def unpack(array):
    shape = jax.ShapeDtypeStruct((128, 2048), BF16)
    outs = call(unpack_kernel, (shape,) * 3, 0, 3 << 20)(array.reshape(16, 3, 128, 128))
    return tuple(v.reshape(2, 1, 64, 2048) for v in outs)


def space_proj_kernel(pos_ref, *refs):
    shards, w_own, w_other, keep, other = refs[:8], refs[8], refs[9], refs[10], refs[11]
    weight = jnp.concatenate([w_own[...], w_other[...]], axis=0)
    for i in range(8):
        at = pos_ref[0] ^ i
        out = nt(shards[i][...], weight).astype(BF16)
        keep[at] = out[:, :128]
        other[at] = out[:, 128:]


def space_proj(pos, shards, w_own, w_other):
    shape = jax.ShapeDtypeStruct((8, 128, 128), BF16)
    vmem = pl.BlockSpec(memory_space=pltpu.VMEM)
    return call(
        space_proj_kernel,
        (shape, shape),
        1 << 30,
        6 << 20,
        in_specs=[pl.BlockSpec(memory_space=pltpu.SMEM)] + [vmem] * 10,
    )(pos, *shards, w_own, w_other)


def time_proj_kernel(pos_ref, *refs):
    shards, weights, out_ref = refs[:4], refs[4:8], refs[8]
    weight = jnp.concatenate([w[...] for w in weights], axis=0)
    for i in range(4):
        at = pos_ref[0] ^ i
        out = nt(shards[i][...], weight).astype(BF16)
        for j in range(4):
            out_ref[lax.rem(pos_ref[1] + j, 4), at] = out[:, j * 128 : (j + 1) * 128]


def time_proj(pos, shards, weights):
    vmem = pl.BlockSpec(memory_space=pltpu.VMEM)
    return call(
        time_proj_kernel,
        jax.ShapeDtypeStruct((4, 4, 128, 128), BF16),
        1 << 30,
        5 << 20,
        in_specs=[pl.BlockSpec(memory_space=pltpu.SMEM)] + [vmem] * 8,
    )(pos, *shards, *weights)


def attend(q, k, v, o, k_t, mask):
    s = nt(k, q)
    if mask is not None:
        s = jnp.where(mask, s, -1e30)
    e = jnp.exp2((s - jnp.max(s, axis=0, keepdims=True)) * (SCALE * LOG2E))
    p = e * (1.0 / jnp.sum(e, axis=0, keepdims=True))
    dv = nn(p.astype(BF16), o)
    dp = nt(v, o)
    delta = jnp.sum(p * dp, axis=0, keepdims=True)
    ds = (p * (dp - delta)).astype(BF16)
    dk = nn(ds, q)
    dq_t = nn(k_t, ds)
    return dq_t, dk, dv


def space_kernel(pos_ref, qkv_ref, keep_ref, got_ref, out_ref, o_ref, dk_ref, dv_ref):
    z_hi = pos_ref[0]
    o_ref[pl.ds(pl.multiple_of(z_hi * 512, 512), 512), :] = keep_ref[...].reshape(512, 128)
    o_ref[pl.ds(pl.multiple_of((1 - z_hi) * 512, 512), 512), :] = got_ref[...].reshape(512, 128)
    k = qkv_ref[:, 1].reshape(1024, 128)
    v = qkv_ref[:, 2].reshape(1024, 128)
    k_t = k.T
    chunk = 256
    for j in range(1024 // chunk):
        n = chunk // 64
        q = qkv_ref[j * n : (j + 1) * n, 0].reshape(chunk, 128)
        o = o_ref[j * chunk : (j + 1) * chunk, :]
        dq_t, dk, dv = attend(q, k, v, o, k_t, None)
        out_ref[j * n : (j + 1) * n, 0] = (dq_t * SCALE).T.astype(BF16).reshape(n, 1, 64, 128)
        if j:
            dk_ref[...] += dk
            dv_ref[...] += dv
        else:
            dk_ref[...] = dk
            dv_ref[...] = dv
    out_ref[:, 1] = (dk_ref[...] * SCALE).astype(BF16).reshape(16, 1, 64, 128)
    out_ref[:, 2] = dv_ref[...].astype(BF16).reshape(16, 1, 64, 128)


def space_attention(z_hi, qkv, keep, got):
    whole = pl.BlockSpec((16, 3, 1, 64, 128), lambda b: (0, 0, b, 0, 0))
    half = pl.BlockSpec((8, 1, 64, 128), lambda b: (0, b, 0, 0))
    return call(
        space_kernel,
        jax.ShapeDtypeStruct((16, 3, 2, 64, 128), BF16),
        5 * (1 << 29),
        4 << 20,
        grid=(2,),
        in_specs=[pl.BlockSpec(memory_space=pltpu.SMEM), whole, half, half],
        out_specs=whole,
        scratch_shapes=[
            pltpu.VMEM((1024, 128), BF16),
            pltpu.VMEM((1024, 128), F32),
            pltpu.VMEM((1024, 128), F32),
        ],
    )(z_hi, qkv, keep, got)


def time_kernel(qkv_ref, o_ref, out_ref):
    rows = lax.broadcasted_iota(jnp.int32, (256, 256), 0)
    columns = lax.broadcasted_iota(jnp.int32, (256, 256), 1)
    mask = ((rows ^ columns) & 15) == 0
    for i in range(4):
        at = slice(16 * i, 16 * (i + 1))
        q = qkv_ref[:, 0, 0, at].reshape(256, 128)
        k = qkv_ref[:, 1, 0, at].reshape(256, 128)
        v = qkv_ref[:, 2, 0, at].reshape(256, 128)
        o = o_ref[:, 0, at].reshape(256, 128)
        dq_t, dk, dv = attend(q, k, v, o, k.T, mask)
        out_ref[:, 0, 0, at] = (dq_t * SCALE).T.astype(BF16).reshape(16, 16, 128)
        out_ref[:, 1, 0, at] = (dk * SCALE).astype(BF16).reshape(16, 16, 128)
        out_ref[:, 2, 0, at] = dv.astype(BF16).reshape(16, 16, 128)


def time_attention(qkv, o):
    whole = pl.BlockSpec((16, 3, 1, 64, 128), lambda b: (0, 0, b, 0, 0))
    return call(
        time_kernel,
        jax.ShapeDtypeStruct((16, 3, 2, 64, 128), BF16),
        5 * (1 << 27),
        4 << 20,
        grid=(2,),
        in_specs=[whole, pl.BlockSpec((16, 1, 64, 128), lambda b: (0, b, 0, 0))],
        out_specs=whole,
    )(qkv, o)


def exchange(array, axis):
    return lax.all_to_all(array, axis, split_axis=0, concat_axis=0, tiled=True)


def on_device(
    query_space,
    key_space,
    value_space,
    query_time,
    key_time,
    value_time,
    block_grad,
    branch_grad,
    proj_space,
    proj_time,
):
    place_s, place_t = lax.axis_index("space"), lax.axis_index("tm")
    z_hi, xc, core = place_s // 8, place_s % 8, place_s % 2
    z_lo, y = place_t // 4, place_t % 4

    time_in = exchange(pack(query_time, key_time, value_time), "tm")

    grad = block_grad.reshape(128, 2048)
    along_x = [grad] + [send(grad, lambda z, x, y, c, k=k: (z, x ^ k, y, c)) for k in (1, 2, 3)]
    pairs = [send(g, lambda z, x, y, c: (z, x, y, 1 - c)) for g in along_x]
    shards = [(along_x, pairs)[i % 2][i // 2] for i in range(8)]
    w_other = send(proj_space, lambda z, x, y, c: (z + (-2 if z % 4 < 2 else 2), x, y, c))
    keep, other = space_proj(xc.reshape(1), shards, proj_space, w_other)
    got = send(other, lambda z, x, y, c: (z + 4, x, y, c))

    space_in = exchange(pack(query_space, key_space, value_space), "space")

    cotangent = (block_grad.astype(F32) + branch_grad.astype(F32)).astype(BF16).reshape(128, 2048)
    along_y = [cotangent] + [
        send(cotangent, lambda z, x, y, c, k=k: (z, x, y ^ k, c)) for k in (1, 2, 3)
    ]
    own_half = lax.dynamic_slice_in_dim(proj_time, core * 64, 64, 0)
    weights = [proj_time]
    for k in (1, 2, 3):
        if k == 2:
            half = send(own_half, lambda z, x, y, c: (z + 2 - 4 * c, x, y, c))
        else:
            half = send(own_half, lambda z, x, y, c, k=k: (z + (1 if k == 3 else -1), x, y, c))
        twin = send(half, lambda z, x, y, c: (z, x, y, 1 - c))
        weights.append(
            jnp.concatenate(
                [jnp.where(core == 0, half, twin), jnp.where(core == 0, twin, half)], axis=0
            )
        )
    out_lines = time_proj(jnp.stack([y, z_lo]), along_y, weights)
    out_lines = lax.all_to_all(
        out_lines,
        "tm",
        split_axis=0,
        concat_axis=0,
        axis_index_groups=[[z * 4 + y for z in range(4)] for y in range(4)],
        tiled=True,
    ).reshape(16, 2, 64, 128)

    space_out = exchange(
        space_attention(
            z_hi.reshape(1), space_in, keep.reshape(8, 2, 64, 128), got.reshape(8, 2, 64, 128)
        ),
        "space",
    )
    time_out = exchange(time_attention(time_in, out_lines), "tm")
    return unpack(space_out) + unpack(time_out)


def solution(mesh):
    tokens = P(None, "tm", "space", None)
    in_specs = (tokens,) * 8 + (P("space", None), P("tm", None))
    return jax.shard_map(
        on_device, mesh=mesh, in_specs=in_specs, out_specs=(tokens,) * 6, check_vma=False
    )
```

```python
import math

import jax
import jax.numpy as jnp
from jax import lax
from jax.experimental import pallas as pl
from jax.experimental.pallas import tpu as pltpu
from jax.sharding import PartitionSpec as P

HEAD_DIM = 128
SCALE = 1.0 / math.sqrt(HEAD_DIM)
LOG2E = math.log2(math.e)
VMEM = 48 * 1024 * 1024
BF16 = jnp.bfloat16
F32 = jnp.float32


def permutation(move):
    pairs = []
    for s in range(16):
        for t in range(16):
            z, x, y, c = (s // 8) * 4 + t // 4, (s // 2) % 4, t % 4, s % 2
            z2, x2, y2, c2 = move(z, x, y, c)
            z2, x2, y2, c2 = z2 % 8, x2 % 4, y2 % 4, c2 % 2
            pairs.append((s * 16 + t, ((z2 // 4) * 8 + x2 * 2 + c2) * 16 + (z2 % 4) * 4 + y2))
    return pairs


def send(array, move):
    return lax.ppermute(array, ("space", "tm"), permutation(move))


def nt(a, b):
    return lax.dot_general(a, b, (((1,), (1,)), ((), ())), preferred_element_type=F32)


def nn(a, b):
    return lax.dot_general(a, b, (((1,), (0,)), ((), ())), preferred_element_type=F32)


def call(kernel, out_shape, flops, size, **kw):
    return pl.pallas_call(
        kernel,
        out_shape=out_shape,
        compiler_params=pltpu.CompilerParams(vmem_limit_bytes=VMEM),
        cost_estimate=pl.CostEstimate(flops=flops, bytes_accessed=size, transcendentals=0),
        **kw,
    )


def pack_kernel(a_ref, b_ref, c_ref, out_ref):
    for t, ref in enumerate((a_ref, b_ref, c_ref)):
        for h in range(16):
            out_ref[h, t] = ref[:, h * 128 : (h + 1) * 128]


def pack(a, b, c):
    flat = [v.reshape(128, 2048) for v in (a, b, c)]
    out = call(pack_kernel, jax.ShapeDtypeStruct((16, 3, 128, 128), BF16), 0, 3 << 20)(*flat)
    return out.reshape(16, 3, 2, 64, 128)


def unpack_kernel(in_ref, a_ref, b_ref, c_ref):
    for t, ref in enumerate((a_ref, b_ref, c_ref)):
        for h in range(16):
            ref[:, h * 128 : (h + 1) * 128] = in_ref[h, t]


def unpack(array):
    shape = jax.ShapeDtypeStruct((128, 2048), BF16)
    outs = call(unpack_kernel, (shape,) * 3, 0, 3 << 20)(array.reshape(16, 3, 128, 128))
    return tuple(v.reshape(2, 1, 64, 2048) for v in outs)


def space_proj_kernel(pos_ref, *refs):
    shards, w_own, w_other, keep, other = refs[:8], refs[8], refs[9], refs[10], refs[11]
    weight = jnp.concatenate([w_own[...], w_other[...]], axis=0)
    for i in range(8):
        at = pos_ref[0] ^ i
        out = nt(shards[i][...], weight).astype(BF16)
        keep[at] = out[:, :128]
        other[at] = out[:, 128:]


def space_proj(pos, shards, w_own, w_other):
    shape = jax.ShapeDtypeStruct((8, 128, 128), BF16)
    vmem = pl.BlockSpec(memory_space=pltpu.VMEM)
    return call(
        space_proj_kernel,
        (shape, shape),
        1 << 30,
        6 << 20,
        in_specs=[pl.BlockSpec(memory_space=pltpu.SMEM)] + [vmem] * 10,
    )(pos, *shards, w_own, w_other)


def time_proj_kernel(pos_ref, *refs):
    shards, own, pieces, outs, weight_ref = refs[:4], refs[4], refs[5:13], refs[13:17], refs[17]
    weight_ref[:128] = own[...]
    for i in range(8):
        for k in range(3):
            row = 128 * (k + 1) + (pos_ref[1] ^ i) * 16
            weight_ref[pl.ds(pl.multiple_of(row, 16), 16)] = pieces[i][k]
    for i in range(4):
        out = nt(shards[i][...], weight_ref[...]).astype(BF16)
        for k in range(4):
            outs[k][pos_ref[0] ^ i] = out[:, k * 128 : (k + 1) * 128]


def time_proj(pos, shards, own, pieces):
    shape = jax.ShapeDtypeStruct((4, 128, 128), BF16)
    vmem = pl.BlockSpec(memory_space=pltpu.VMEM)
    return call(
        time_proj_kernel,
        (shape,) * 4,
        1 << 30,
        5 << 20,
        in_specs=[pl.BlockSpec(memory_space=pltpu.SMEM)] + [vmem] * 13,
        scratch_shapes=[pltpu.VMEM((512, 2048), BF16)],
    )(pos, *shards, own, *pieces)


def attend(q, k, v, o, k_t, mask):
    s = nt(k, q)
    if mask is not None:
        s = jnp.where(mask, s, -1e30)
    e = jnp.exp2((s - jnp.max(s, axis=0, keepdims=True)) * (SCALE * LOG2E))
    p = e * (1.0 / jnp.sum(e, axis=0, keepdims=True))
    dv = nn(p.astype(BF16), o)
    dp = nt(v, o)
    delta = jnp.sum(p * dp, axis=0, keepdims=True)
    ds = (p * (dp - delta)).astype(BF16)
    dk = nn(ds, q)
    dq_t = nn(k_t, ds)
    return dq_t, dk, dv


def space_kernel(pos_ref, qkv_ref, keep_ref, got_ref, out_ref, o_ref, dk_ref, dv_ref):
    z_hi = pos_ref[0]
    o_ref[pl.ds(pl.multiple_of(z_hi * 512, 512), 512), :] = keep_ref[...].reshape(512, 128)
    o_ref[pl.ds(pl.multiple_of((1 - z_hi) * 512, 512), 512), :] = got_ref[...].reshape(512, 128)
    k = qkv_ref[:, 1].reshape(1024, 128)
    v = qkv_ref[:, 2].reshape(1024, 128)
    k_t = k.T
    chunk = 256
    for j in range(1024 // chunk):
        n = chunk // 64
        q = qkv_ref[j * n : (j + 1) * n, 0].reshape(chunk, 128)
        o = o_ref[j * chunk : (j + 1) * chunk, :]
        dq_t, dk, dv = attend(q, k, v, o, k_t, None)
        out_ref[j * n : (j + 1) * n, 0] = (dq_t * SCALE).T.astype(BF16).reshape(n, 1, 64, 128)
        if j:
            dk_ref[...] += dk
            dv_ref[...] += dv
        else:
            dk_ref[...] = dk
            dv_ref[...] = dv
    out_ref[:, 1] = (dk_ref[...] * SCALE).astype(BF16).reshape(16, 1, 64, 128)
    out_ref[:, 2] = dv_ref[...].astype(BF16).reshape(16, 1, 64, 128)


def space_attention(z_hi, qkv, keep, got):
    whole = pl.BlockSpec((16, 3, 1, 64, 128), lambda b: (0, 0, b, 0, 0))
    half = pl.BlockSpec((8, 1, 64, 128), lambda b: (0, b, 0, 0))
    return call(
        space_kernel,
        jax.ShapeDtypeStruct((16, 3, 2, 64, 128), BF16),
        5 * (1 << 29),
        4 << 20,
        grid=(2,),
        in_specs=[pl.BlockSpec(memory_space=pltpu.SMEM), whole, half, half],
        out_specs=whole,
        scratch_shapes=[
            pltpu.VMEM((1024, 128), BF16),
            pltpu.VMEM((1024, 128), F32),
            pltpu.VMEM((1024, 128), F32),
        ],
    )(z_hi, qkv, keep, got)


def time_kernel(pos_ref, qkv_ref, *refs):
    parts, out_ref, o_ref = refs[:4], refs[4], refs[5]
    for i in range(4):
        o_ref[pl.ds(((pos_ref[0] - i) & 3) * 4, 4)] = parts[i][:, 0]
    rows = lax.broadcasted_iota(jnp.int32, (256, 256), 0)
    columns = lax.broadcasted_iota(jnp.int32, (256, 256), 1)
    mask = ((rows ^ columns) & 15) == 0
    for i in range(4):
        at = slice(16 * i, 16 * (i + 1))
        q = qkv_ref[:, 0, 0, at].reshape(256, 128)
        k = qkv_ref[:, 1, 0, at].reshape(256, 128)
        v = qkv_ref[:, 2, 0, at].reshape(256, 128)
        o = o_ref[:, at].reshape(256, 128)
        dq_t, dk, dv = attend(q, k, v, o, k.T, mask)
        out_ref[:, 0, 0, at] = (dq_t * SCALE).T.astype(BF16).reshape(16, 16, 128)
        out_ref[:, 1, 0, at] = (dk * SCALE).astype(BF16).reshape(16, 16, 128)
        out_ref[:, 2, 0, at] = dv.astype(BF16).reshape(16, 16, 128)


def time_attention(z_lo, qkv, parts):
    whole = pl.BlockSpec((16, 3, 1, 64, 128), lambda b: (0, 0, b, 0, 0))
    quarter = pl.BlockSpec((4, 1, 64, 128), lambda b: (0, b, 0, 0))
    return call(
        time_kernel,
        jax.ShapeDtypeStruct((16, 3, 2, 64, 128), BF16),
        5 * (1 << 27),
        4 << 20,
        grid=(2,),
        in_specs=[pl.BlockSpec(memory_space=pltpu.SMEM), whole] + [quarter] * 4,
        out_specs=whole,
        scratch_shapes=[pltpu.VMEM((16, 64, 128), BF16)],
    )(z_lo, qkv, *parts)


def exchange(array, axis):
    return lax.all_to_all(array, axis, split_axis=0, concat_axis=0, tiled=True)


def on_device(
    query_space,
    key_space,
    value_space,
    query_time,
    key_time,
    value_time,
    block_grad,
    branch_grad,
    proj_space,
    proj_time,
):
    place_s, place_t = lax.axis_index("space"), lax.axis_index("tm")
    z_hi, xc = place_s // 8, place_s % 8
    z_lo, y = place_t // 4, place_t % 4

    time_in = exchange(pack(query_time, key_time, value_time), "tm")

    rows = lax.dynamic_slice_in_dim(proj_time, xc * 16, 16, 0)
    piece = jnp.stack(
        [
            send(rows, lambda z, x, y, c: (z - 1, x, y, c)),
            send(rows, lambda z, x, y, c: (z + 2 - 4 * c, x, y, c)),
            send(rows, lambda z, x, y, c: (z + 1, x, y, c)),
        ]
    )
    along_x = [piece] + [send(piece, lambda z, x, y, c, k=k: (z, x ^ k, y, c)) for k in (1, 2, 3)]
    twins = [send(p, lambda z, x, y, c: (z, x, y, 1 - c)) for p in along_x]
    pieces = [(along_x, twins)[i % 2][i // 2] for i in range(8)]

    cotangent = (block_grad.astype(F32) + branch_grad.astype(F32)).astype(BF16).reshape(128, 2048)
    along_y = [cotangent] + [
        send(cotangent, lambda z, x, y, c, k=k: (z, x, y ^ k, c)) for k in (1, 2, 3)
    ]

    grad = block_grad.reshape(128, 2048)
    along_x = [grad] + [send(grad, lambda z, x, y, c, k=k: (z, x ^ k, y, c)) for k in (1, 2, 3)]
    twins = [send(g, lambda z, x, y, c: (z, x, y, 1 - c)) for g in along_x]
    shards = [(along_x, twins)[i % 2][i // 2] for i in range(8)]
    w_other = send(proj_space, lambda z, x, y, c: (z + (-2 if z % 4 < 2 else 2), x, y, c))

    space_packed = pack(query_space, key_space, value_space)
    time_in, pieces, along_y, shards, w_other, space_packed = lax.optimization_barrier(
        (time_in, pieces, along_y, shards, w_other, space_packed)
    )

    space_in = exchange(space_packed, "space")
    outs = time_proj(jnp.stack([y, xc]), along_y, proj_time, pieces)
    parts = [outs[0]] + [
        lax.ppermute(
            outs[k], "tm", [(t, (t // 4 + k) % 4 * 4 + t % 4) for t in range(16)]
        )
        for k in (1, 2, 3)
    ]
    keep, other = space_proj(xc.reshape(1), shards, proj_space, w_other)
    got = send(other, lambda z, x, y, c: (z + 4, x, y, c))
    time_grads = time_attention(
        z_lo.reshape(1), time_in, [p.reshape(4, 2, 64, 128) for p in parts]
    )
    space_in, keep, got, time_grads = lax.optimization_barrier((space_in, keep, got, time_grads))

    time_out = exchange(time_grads, "tm")
    space_grads = space_attention(
        z_hi.reshape(1), space_in, keep.reshape(8, 2, 64, 128), got.reshape(8, 2, 64, 128)
    )
    time_out, space_grads = lax.optimization_barrier((time_out, space_grads))
    space_out = exchange(space_grads, "space")
    return unpack(space_out) + unpack(time_out)


def solution(mesh):
    tokens = P(None, "tm", "space", None)
    in_specs = (tokens,) * 8 + (P("space", None), P("tm", None))
    return jax.shard_map(
        on_device, mesh=mesh, in_specs=in_specs, out_specs=(tokens,) * 6, check_vma=False
    )
```

```python
import math

import jax
import jax.numpy as jnp
from jax import lax
from jax.experimental import pallas as pl
from jax.experimental.pallas import tpu as pltpu
from jax.sharding import PartitionSpec as P

HEAD_DIM = 128
SCALE = 1.0 / math.sqrt(HEAD_DIM)
LOG2E = math.log2(math.e)
VMEM = 48 * 1024 * 1024
BF16 = jnp.bfloat16
F32 = jnp.float32
WHOLE = pl.BlockSpec(memory_space=pltpu.VMEM)
SCALARS = pl.BlockSpec(memory_space=pltpu.SMEM)
LATER = pl.BlockSpec(memory_space=pl.ANY)


def permutation(move):
    pairs = []
    for s in range(16):
        for t in range(16):
            z, x, y, c = (s // 8) * 4 + t // 4, (s // 2) % 4, t % 4, s % 2
            z2, x2, y2, c2 = move(z, x, y, c)
            z2, x2, y2, c2 = z2 % 8, x2 % 4, y2 % 4, c2 % 2
            pairs.append((s * 16 + t, ((z2 // 4) * 8 + x2 * 2 + c2) * 16 + (z2 % 4) * 4 + y2))
    return pairs


def send(array, move):
    return lax.ppermute(array, ("space", "tm"), permutation(move))


def nt(a, b):
    return lax.dot_general(a, b, (((1,), (1,)), ((), ())), preferred_element_type=F32)


def nn(a, b):
    return lax.dot_general(a, b, (((1,), (0,)), ((), ())), preferred_element_type=F32)


def call(kernel, out_shape, flops, size, **kw):
    return pl.pallas_call(
        kernel,
        out_shape=out_shape,
        compiler_params=pltpu.CompilerParams(vmem_limit_bytes=VMEM),
        cost_estimate=pl.CostEstimate(flops=flops, bytes_accessed=size, transcendentals=0),
        **kw,
    )


def pack_kernel(a_ref, b_ref, c_ref, *refs):
    out_ref = refs[-1]
    for t, ref in enumerate((a_ref, b_ref, c_ref)):
        for h in range(16):
            out_ref[h, t] = ref[:, h * 128 : (h + 1) * 128]


def pack(a, b, c, *after):
    flat = [v.reshape(128, 2048) for v in (a, b, c)]
    out = call(
        pack_kernel,
        jax.ShapeDtypeStruct((16, 3, 128, 128), BF16),
        0,
        3 << 20,
        in_specs=[WHOLE] * 3 + [LATER] * len(after),
    )(*flat, *after)
    return out.reshape(16, 3, 2, 64, 128)


def unpack_kernel(in_ref, a_ref, b_ref, c_ref):
    for t, ref in enumerate((a_ref, b_ref, c_ref)):
        for h in range(16):
            ref[:, h * 128 : (h + 1) * 128] = in_ref[h, t]


def unpack(array):
    shape = jax.ShapeDtypeStruct((128, 2048), BF16)
    outs = call(unpack_kernel, (shape,) * 3, 0, 3 << 20)(array.reshape(16, 3, 128, 128))
    return tuple(v.reshape(2, 1, 64, 2048) for v in outs)


def space_proj_kernel(shards_ref, w_own, w_other, after_ref, keep, other):
    weight = jnp.concatenate([w_own[...], w_other[...]], axis=0)
    for i in range(8):
        out = nt(shards_ref[i], weight).astype(BF16)
        keep[i] = out[:, :128]
        other[i] = out[:, 128:]


def space_proj(shards, w_own, w_other, after):
    shape = jax.ShapeDtypeStruct((8, 128, 128), BF16)
    return call(
        space_proj_kernel,
        (shape, shape),
        1 << 30,
        6 << 20,
        in_specs=[WHOLE] * 3 + [LATER],
    )(shards, w_own, w_other, after)


def time_proj_kernel(y_ref, *refs):
    shards, own, pieces_ref, outs, weight_ref = refs[:4], refs[4], refs[5], refs[6:10], refs[10]
    weight_ref[:128] = own[...]
    for i in range(8):
        for k in range(3):
            weight_ref[128 * (k + 1) + 16 * i : 128 * (k + 1) + 16 * (i + 1)] = pieces_ref[i, k]
    for i in range(4):
        out = nt(shards[i][...], weight_ref[...]).astype(BF16)
        for k in range(4):
            outs[k][y_ref[0] ^ i] = out[:, k * 128 : (k + 1) * 128]


def time_proj(y, shards, own, pieces):
    shape = jax.ShapeDtypeStruct((4, 128, 128), BF16)
    return call(
        time_proj_kernel,
        (shape,) * 4,
        1 << 30,
        5 << 20,
        in_specs=[SCALARS] + [WHOLE] * 6,
        scratch_shapes=[pltpu.VMEM((512, 2048), BF16)],
    )(y, *shards, own, pieces)


def attend(q, k, v, o, k_t, mask):
    s = nt(k, q)
    if mask is not None:
        s = jnp.where(mask, s, -1e30)
    e = jnp.exp2((s - jnp.max(s, axis=0, keepdims=True)) * (SCALE * LOG2E))
    p = e * (1.0 / jnp.sum(e, axis=0, keepdims=True))
    dv = nn(p.astype(BF16), o)
    dp = nt(v, o)
    delta = jnp.sum(p * dp, axis=0, keepdims=True)
    ds = (p * (dp - delta)).astype(BF16)
    dk = nn(ds, q)
    dq_t = nn(k_t, ds)
    return dq_t, dk, dv


def space_kernel(pos_ref, qkv_ref, keep_ref, got_ref, after_ref, out_ref, o_ref, dk_ref, dv_ref):
    z_hi = pos_ref[0]
    o_ref[pl.ds(pl.multiple_of(z_hi * 512, 512), 512), :] = keep_ref[...].reshape(512, 128)
    o_ref[pl.ds(pl.multiple_of((1 - z_hi) * 512, 512), 512), :] = got_ref[...].reshape(512, 128)
    k = qkv_ref[:, 1].reshape(1024, 128)
    v = qkv_ref[:, 2].reshape(1024, 128)
    k_t = k.T
    chunk = 256
    for j in range(1024 // chunk):
        n = chunk // 64
        q = qkv_ref[j * n : (j + 1) * n, 0].reshape(chunk, 128)
        o = o_ref[j * chunk : (j + 1) * chunk, :]
        dq_t, dk, dv = attend(q, k, v, o, k_t, None)
        out_ref[j * n : (j + 1) * n, 0] = (dq_t * SCALE).T.astype(BF16).reshape(n, 1, 64, 128)
        if j:
            dk_ref[...] += dk
            dv_ref[...] += dv
        else:
            dk_ref[...] = dk
            dv_ref[...] = dv
    out_ref[:, 1] = (dk_ref[...] * SCALE).astype(BF16).reshape(16, 1, 64, 128)
    out_ref[:, 2] = dv_ref[...].astype(BF16).reshape(16, 1, 64, 128)


def space_attention(z_hi, qkv, keep, got, after):
    whole = pl.BlockSpec((16, 3, 1, 64, 128), lambda b: (0, 0, b, 0, 0))
    half = pl.BlockSpec((8, 1, 64, 128), lambda b: (0, b, 0, 0))
    return call(
        space_kernel,
        jax.ShapeDtypeStruct((16, 3, 2, 64, 128), BF16),
        5 * (1 << 29),
        4 << 20,
        grid=(2,),
        in_specs=[SCALARS, whole, half, half, LATER],
        out_specs=whole,
        scratch_shapes=[
            pltpu.VMEM((1024, 128), BF16),
            pltpu.VMEM((1024, 128), F32),
            pltpu.VMEM((1024, 128), F32),
        ],
    )(z_hi, qkv, keep, got, after)


def time_kernel(pos_ref, qkv_ref, *refs):
    parts, out_ref, o_ref = refs[:4], refs[4], refs[5]
    for i in range(4):
        o_ref[pl.ds(((pos_ref[0] - i) & 3) * 4, 4)] = parts[i][:, 0]
    rows = lax.broadcasted_iota(jnp.int32, (256, 256), 0)
    columns = lax.broadcasted_iota(jnp.int32, (256, 256), 1)
    mask = ((rows ^ columns) & 15) == 0
    for i in range(4):
        at = slice(16 * i, 16 * (i + 1))
        q = qkv_ref[:, 0, 0, at].reshape(256, 128)
        k = qkv_ref[:, 1, 0, at].reshape(256, 128)
        v = qkv_ref[:, 2, 0, at].reshape(256, 128)
        o = o_ref[:, at].reshape(256, 128)
        dq_t, dk, dv = attend(q, k, v, o, k.T, mask)
        out_ref[:, 0, 0, at] = (dq_t * SCALE).T.astype(BF16).reshape(16, 16, 128)
        out_ref[:, 1, 0, at] = (dk * SCALE).astype(BF16).reshape(16, 16, 128)
        out_ref[:, 2, 0, at] = dv.astype(BF16).reshape(16, 16, 128)


def time_attention(z_lo, qkv, parts):
    whole = pl.BlockSpec((16, 3, 1, 64, 128), lambda b: (0, 0, b, 0, 0))
    quarter = pl.BlockSpec((4, 1, 64, 128), lambda b: (0, b, 0, 0))
    return call(
        time_kernel,
        jax.ShapeDtypeStruct((16, 3, 2, 64, 128), BF16),
        5 * (1 << 27),
        4 << 20,
        grid=(2,),
        in_specs=[SCALARS, whole] + [quarter] * 4,
        out_specs=whole,
        scratch_shapes=[pltpu.VMEM((16, 64, 128), BF16)],
    )(z_lo, qkv, *parts)


def exchange(array, axis):
    return lax.all_to_all(array, axis, split_axis=0, concat_axis=0, tiled=True)


def on_device(
    query_space,
    key_space,
    value_space,
    query_time,
    key_time,
    value_time,
    block_grad,
    branch_grad,
    proj_space,
    proj_time,
):
    place_s, place_t = lax.axis_index("space"), lax.axis_index("tm")
    z_hi, xc = place_s // 8, place_s % 8
    z_lo, y = place_t // 4, place_t % 4

    halves = [[z * 8 + i for i in range(8)] for z in range(2)]
    shards = lax.all_gather(block_grad.reshape(128, 2048), "space", axis_index_groups=halves)
    rows = lax.dynamic_slice_in_dim(proj_time, xc * 16, 16, 0)
    time_packed = pack(query_time, key_time, value_time, rows)
    time_in = exchange(time_packed, "tm")
    w_other = send(proj_space, lambda z, x, y, c: (z + (-2 if z % 4 < 2 else 2), x, y, c))
    piece = jnp.stack(
        [
            send(rows, lambda z, x, y, c: (z - 1, x, y, c)),
            send(rows, lambda z, x, y, c: (z + 2 - 4 * c, x, y, c)),
            send(rows, lambda z, x, y, c: (z + 1, x, y, c)),
        ]
    )

    space_packed = pack(query_space, key_space, value_space, time_in, w_other)
    space_in = exchange(space_packed, "space")
    keep, other = space_proj(shards, proj_space, w_other, space_packed)
    got = send(other, lambda z, x, y, c: (z + 4, x, y, c))
    pieces = lax.all_gather(piece, "space", axis_index_groups=halves)
    cotangent = (block_grad.astype(F32) + branch_grad.astype(F32)).astype(BF16).reshape(128, 2048)
    along_y = [cotangent] + [
        send(cotangent, lambda z, x, y, c, k=k: (z, x, y ^ k, c)) for k in (1, 2, 3)
    ]
    outs = time_proj(y.reshape(1), along_y, proj_time, pieces)

    parts = [outs[0]] + [
        lax.ppermute(outs[k], "tm", [(t, (t // 4 + k) % 4 * 4 + t % 4) for t in range(16)])
        for k in (1, 2, 3)
    ]
    space_grads = space_attention(
        z_hi.reshape(1),
        space_in,
        keep.reshape(8, 2, 64, 128),
        got.reshape(8, 2, 64, 128),
        outs[0],
    )
    space_grads, parts = lax.optimization_barrier((space_grads, parts))

    space_out = exchange(space_grads, "space")
    time_grads = time_attention(
        z_lo.reshape(1), time_in, [p.reshape(4, 2, 64, 128) for p in parts]
    )
    space_out, time_grads = lax.optimization_barrier((space_out, time_grads))
    time_out = exchange(time_grads, "tm")
    return unpack(space_out) + unpack(time_out)


def solution(mesh):
    tokens = P(None, "tm", "space", None)
    in_specs = (tokens,) * 8 + (P("space", None), P("tm", None))
    return jax.shard_map(
        on_device, mesh=mesh, in_specs=in_specs, out_specs=(tokens,) * 6, check_vma=False
    )
```

```python
import math

import jax
import jax.numpy as jnp
from jax import lax
from jax.experimental import pallas as pl
from jax.experimental.pallas import tpu as pltpu
from jax.sharding import PartitionSpec as P

HEAD_DIM = 128
SCALE = 1.0 / math.sqrt(HEAD_DIM)
LOG2E = math.log2(math.e)
VMEM = 48 * 1024 * 1024
BF16 = jnp.bfloat16
F32 = jnp.float32
WHOLE = pl.BlockSpec(memory_space=pltpu.VMEM)
SCALARS = pl.BlockSpec(memory_space=pltpu.SMEM)
LATER = pl.BlockSpec(memory_space=pl.ANY)
IN_HBM = pl.BlockSpec(memory_space=pltpu.HBM)


def permutation(move):
    pairs = []
    for s in range(16):
        for t in range(16):
            z, x, y, c = (s // 8) * 4 + t // 4, (s // 2) % 4, t % 4, s % 2
            z2, x2, y2, c2 = move(z, x, y, c)
            z2, x2, y2, c2 = z2 % 8, x2 % 4, y2 % 4, c2 % 2
            pairs.append((s * 16 + t, ((z2 // 4) * 8 + x2 * 2 + c2) * 16 + (z2 % 4) * 4 + y2))
    return pairs


def send(array, move):
    return lax.ppermute(array, ("space", "tm"), permutation(move))


def twin(array):
    return send(array, lambda z, x, y, c: (z, x, y, 1 - c))


def nt(a, b):
    return lax.dot_general(a, b, (((1,), (1,)), ((), ())), preferred_element_type=F32)


def nn(a, b):
    return lax.dot_general(a, b, (((1,), (0,)), ((), ())), preferred_element_type=F32)


def call(kernel, out_shape, flops, size, **kw):
    return pl.pallas_call(
        kernel,
        out_shape=out_shape,
        compiler_params=pltpu.CompilerParams(vmem_limit_bytes=VMEM),
        cost_estimate=pl.CostEstimate(flops=flops, bytes_accessed=size, transcendentals=0),
        **kw,
    )


def pack_kernel(a_ref, b_ref, c_ref, *refs):
    out_ref, sems = refs[-2:]
    copies = [
        pltpu.make_async_copy(ref.at[:, h * 128 : (h + 1) * 128], out_ref.at[h, t], sems.at[t, h])
        for h in range(16)
        for t, ref in enumerate((a_ref, b_ref, c_ref))
    ]
    for copy in copies:
        copy.start()
    for copy in copies:
        copy.wait()


def pack(a, b, c, *after):
    flat = [v.reshape(128, 2048) for v in (a, b, c)]
    out = call(
        pack_kernel,
        jax.ShapeDtypeStruct((16, 3, 128, 128), BF16),
        0,
        3 << 20,
        in_specs=[IN_HBM] * 3 + [WHOLE] * len(after),
        out_specs=WHOLE,
        scratch_shapes=[pltpu.SemaphoreType.DMA((3, 16))],
    )(*flat, *after)
    return out.reshape(16, 3, 2, 64, 128)


def unpack_kernel(in_ref, a_ref, b_ref, c_ref):
    for t, ref in enumerate((a_ref, b_ref, c_ref)):
        for h in range(16):
            ref[:, h * 128 : (h + 1) * 128] = in_ref[h, t]


def unpack(array):
    shape = jax.ShapeDtypeStruct((128, 2048), BF16)
    outs = call(unpack_kernel, (shape,) * 3, 0, 3 << 20)(array.reshape(16, 3, 128, 128))
    return tuple(v.reshape(2, 1, 64, 2048) for v in outs)


def rows_kernel(at_ref, space_ref, time_ref, rows_ref, both_ref, sems):
    half = space_ref.at[pl.ds(pl.multiple_of(at_ref[0] * 64, 64), 64), :]
    rows = time_ref.at[pl.ds(pl.multiple_of(at_ref[1] * 64, 64), 64), :]
    quarter = time_ref.at[pl.ds(pl.multiple_of(at_ref[2] * 32, 32), 32), :]
    copies = [
        pltpu.make_async_copy(rows, rows_ref, sems.at[0]),
        pltpu.make_async_copy(half, both_ref.at[:64], sems.at[1]),
        pltpu.make_async_copy(quarter, both_ref.at[64:], sems.at[2]),
    ]
    for copy in copies:
        copy.start()
    for copy in copies:
        copy.wait()


def rows_to_send(at, proj_space, proj_time):
    return call(
        rows_kernel,
        (jax.ShapeDtypeStruct((64, 2048), BF16), jax.ShapeDtypeStruct((96, 2048), BF16)),
        0,
        1 << 20,
        in_specs=[SCALARS] + [IN_HBM] * 2,
        out_specs=(WHOLE, WHOLE),
        scratch_shapes=[pltpu.SemaphoreType.DMA((3,))],
    )(at, proj_space, proj_time)


def gathered_kernel(both_ref, rows_ref, half_ref, along_z_ref):
    half_ref[...] = both_ref[:64]
    along_z_ref[:64] = rows_ref[...]
    along_z_ref[64:] = both_ref[64:]


def gathered(both, rows):
    return call(
        gathered_kernel,
        (jax.ShapeDtypeStruct((64, 2048), BF16), jax.ShapeDtypeStruct((96, 2048), BF16)),
        0,
        1 << 20,
        in_specs=[WHOLE] * 2,
    )(both, rows)


def pair_kernel(a_ref, b_ref, *refs):
    out_ref = refs[-1]
    out_ref[0] = a_ref[...]
    out_ref[1] = b_ref[...]


def pair(a, b, *after):
    shape = jax.ShapeDtypeStruct((2, 96, 2048), BF16)
    return call(pair_kernel, shape, 0, 1 << 20, in_specs=[WHOLE] * (2 + len(after)))(a, b, *after)


def stack_kernel(a_ref, b_ref, c_ref, d_ref, out_ref):
    for i, ref in enumerate((a_ref, b_ref, c_ref, d_ref)):
        out_ref[i] = ref[...]


def stacked(shards):
    shape = jax.ShapeDtypeStruct((4, 128, 2048), BF16)
    return call(stack_kernel, shape, 0, 4 << 20, in_specs=[WHOLE] * 4)(*shards)


def space_proj_kernel(at_ref, *refs):
    own_ref, twin_ref, w_own, w_half, w_rest = refs[:5]
    keep, other, weight_ref = refs[-3:]
    weight_ref[:128] = w_own[...]
    first = 128 + at_ref[1] * 64
    rest = 128 + (1 - at_ref[1]) * 64
    weight_ref[pl.ds(pl.multiple_of(first, 64), 64)] = w_half[...]
    weight_ref[pl.ds(pl.multiple_of(rest, 64), 64)] = w_rest[...]
    for i in range(8):
        at = at_ref[0] ^ i
        out = nt((own_ref, twin_ref)[i % 2][i // 2], weight_ref[...]).astype(BF16)
        keep[at] = out[:, :128]
        other[at] = out[:, 128:]


def space_proj(at, own, twins, w_own, w_half, w_rest, *after):
    shape = jax.ShapeDtypeStruct((8, 128, 128), BF16)
    return call(
        space_proj_kernel,
        (shape, shape),
        1 << 30,
        6 << 20,
        in_specs=[SCALARS] + [WHOLE] * (5 + len(after)),
        scratch_shapes=[pltpu.VMEM((256, 2048), BF16)],
    )(at, own, twins, w_own, w_half, w_rest, *after)


def time_proj_kernel(at_ref, *refs):
    shards, own, pieces, outs, weight_ref = refs[:4], refs[4], refs[5:7], refs[7:11], refs[11]
    weight_ref[:128] = own[...]
    for i in range(4):
        quarter = at_ref[1] ^ i
        core, half = quarter & 1, quarter >> 1
        row = 128 * (3 - 2 * core) + 64 * half
        weight_ref[pl.ds(pl.multiple_of(row, 64), 64)] = pieces[i % 2][i // 2, :64]
        row = 256 + 32 * quarter
        weight_ref[pl.ds(pl.multiple_of(row, 32), 32)] = pieces[i % 2][i // 2, 64:]
    for i in range(4):
        out = nt(shards[i][...], weight_ref[...]).astype(BF16)
        for k in range(4):
            outs[k][at_ref[0] ^ i] = out[:, k * 128 : (k + 1) * 128]


def time_proj(at, shards, own, rows, twin_rows):
    shape = jax.ShapeDtypeStruct((4, 128, 128), BF16)
    return call(
        time_proj_kernel,
        (shape,) * 4,
        1 << 30,
        5 << 20,
        in_specs=[SCALARS] + [WHOLE] * 7,
        scratch_shapes=[pltpu.VMEM((512, 2048), BF16)],
    )(at, *shards, own, rows, twin_rows)


def attend(q, k, v, o, k_t, mask):
    s = nt(k, q)
    if mask is not None:
        s = jnp.where(mask, s, -1e30)
    e = jnp.exp2((s - jnp.max(s, axis=0, keepdims=True)) * (SCALE * LOG2E))
    p = e * (1.0 / jnp.sum(e, axis=0, keepdims=True))
    dv = nn(p.astype(BF16), o)
    dp = nt(v, o)
    delta = jnp.sum(p * dp, axis=0, keepdims=True)
    ds = (p * (dp - delta)).astype(BF16)
    dk = nn(ds, q)
    dq_t = nn(k_t, ds)
    return dq_t, dk, dv


def space_kernel(pos_ref, qkv_ref, keep_ref, got_ref, after_ref, out_ref, o_ref, dk_ref, dv_ref):
    z_hi = pos_ref[0]
    o_ref[pl.ds(pl.multiple_of(z_hi * 512, 512), 512), :] = keep_ref[...].reshape(512, 128)
    o_ref[pl.ds(pl.multiple_of((1 - z_hi) * 512, 512), 512), :] = got_ref[...].reshape(512, 128)
    k = qkv_ref[:, 1].reshape(1024, 128)
    v = qkv_ref[:, 2].reshape(1024, 128)
    k_t = k.T
    chunk = 256
    for j in range(1024 // chunk):
        n = chunk // 64
        q = qkv_ref[j * n : (j + 1) * n, 0].reshape(chunk, 128)
        o = o_ref[j * chunk : (j + 1) * chunk, :]
        dq_t, dk, dv = attend(q, k, v, o, k_t, None)
        out_ref[j * n : (j + 1) * n, 0] = (dq_t * SCALE).T.astype(BF16).reshape(n, 1, 64, 128)
        if j:
            dk_ref[...] += dk
            dv_ref[...] += dv
        else:
            dk_ref[...] = dk
            dv_ref[...] = dv
    out_ref[:, 1] = (dk_ref[...] * SCALE).astype(BF16).reshape(16, 1, 64, 128)
    out_ref[:, 2] = dv_ref[...].astype(BF16).reshape(16, 1, 64, 128)


def space_attention(z_hi, qkv, keep, got, after):
    whole = pl.BlockSpec((16, 3, 1, 64, 128), lambda b: (0, 0, b, 0, 0))
    half = pl.BlockSpec((8, 1, 64, 128), lambda b: (0, b, 0, 0))
    return call(
        space_kernel,
        jax.ShapeDtypeStruct((16, 3, 2, 64, 128), BF16),
        5 * (1 << 29),
        4 << 20,
        grid=(2,),
        in_specs=[SCALARS, whole, half, half, LATER],
        out_specs=whole,
        scratch_shapes=[
            pltpu.VMEM((1024, 128), BF16),
            pltpu.VMEM((1024, 128), F32),
            pltpu.VMEM((1024, 128), F32),
        ],
    )(z_hi, qkv, keep, got, after)


def time_kernel(pos_ref, qkv_ref, *refs):
    parts, out_ref, o_ref = refs[:4], refs[4], refs[5]
    for i in range(4):
        o_ref[pl.ds(((pos_ref[0] - i) & 3) * 4, 4)] = parts[i][:, 0]
    rows = lax.broadcasted_iota(jnp.int32, (256, 256), 0)
    columns = lax.broadcasted_iota(jnp.int32, (256, 256), 1)
    mask = ((rows ^ columns) & 15) == 0
    for i in range(4):
        at = slice(16 * i, 16 * (i + 1))
        q = qkv_ref[:, 0, 0, at].reshape(256, 128)
        k = qkv_ref[:, 1, 0, at].reshape(256, 128)
        v = qkv_ref[:, 2, 0, at].reshape(256, 128)
        o = o_ref[:, at].reshape(256, 128)
        dq_t, dk, dv = attend(q, k, v, o, k.T, mask)
        out_ref[:, 0, 0, at] = (dq_t * SCALE).T.astype(BF16).reshape(16, 16, 128)
        out_ref[:, 1, 0, at] = (dk * SCALE).astype(BF16).reshape(16, 16, 128)
        out_ref[:, 2, 0, at] = dv.astype(BF16).reshape(16, 16, 128)


def time_attention(z_lo, qkv, parts):
    whole = pl.BlockSpec((16, 3, 1, 64, 128), lambda b: (0, 0, b, 0, 0))
    quarter = pl.BlockSpec((4, 1, 64, 128), lambda b: (0, b, 0, 0))
    return call(
        time_kernel,
        jax.ShapeDtypeStruct((16, 3, 2, 64, 128), BF16),
        5 * (1 << 27),
        4 << 20,
        grid=(2,),
        in_specs=[SCALARS, whole] + [quarter] * 4,
        out_specs=whole,
        scratch_shapes=[pltpu.VMEM((16, 64, 128), BF16)],
    )(z_lo, qkv, *parts)


def exchange(array, axis):
    return lax.all_to_all(array, axis, split_axis=0, concat_axis=0, tiled=True)


def on_device(
    query_space,
    key_space,
    value_space,
    query_time,
    key_time,
    value_time,
    block_grad,
    branch_grad,
    proj_space,
    proj_time,
):
    place_s, place_t = lax.axis_index("space"), lax.axis_index("tm")
    z_hi, xc = place_s // 8, place_s % 8
    z_lo, y = place_t // 4, place_t % 4

    time_in = exchange(pack(query_time, key_time, value_time), "tm")
    grad = block_grad.reshape(128, 2048)
    along_x = stacked(
        [grad] + [send(grad, lambda z, x, y, c, k=k: (z, x ^ k, y, c)) for k in (1, 2, 3)]
    )
    half = xc // 2 % 2
    rows, both = rows_to_send(jnp.stack([y % 2, half, xc % 4]), proj_space, proj_time)
    both = send(both, lambda z, x, y, c: (z + (-2 if z % 4 < 2 else 2), x, y, c))
    rows = send(rows, lambda z, x, y, c: (z + 1 - 2 * c, x, y, c))
    w_half, along_z = gathered(both, rows)
    cotangent = (block_grad.astype(F32) + branch_grad.astype(F32)).astype(BF16).reshape(128, 2048)
    along_y = [cotangent] + [
        send(cotangent, lambda z, x, y, c, k=k: (z, x, y ^ k, c)) for k in (1, 2, 3)
    ]

    space_packed = pack(
        query_space, key_space, value_space, along_x, w_half, along_z, along_y[1]
    )
    space_packed, time_in = lax.optimization_barrier((space_packed, time_in))
    space_in = exchange(space_packed, "space")
    w_rest = send(w_half, lambda z, x, y, c: (z, x, y ^ 1, c))
    along_z2 = send(along_z, lambda z, x, y, c: (z, x ^ 1, y, c))
    keep, other = space_proj(
        jnp.stack([xc, y % 2]),
        along_x,
        twin(along_x),
        proj_space,
        w_half,
        w_rest,
        along_y[2],
    )
    got = send(other, lambda z, x, y, c: (z + 4, x, y, c))
    pieces = pair(along_z, along_z2, keep, along_y[3])
    outs = time_proj(jnp.stack([y, xc % 4]), along_y, proj_time, pieces, twin(pieces))

    parts = [outs[0]] + [
        lax.ppermute(outs[k], "tm", [(t, (t // 4 + k) % 4 * 4 + t % 4) for t in range(16)])
        for k in (1, 2, 3)
    ]
    space_grads = space_attention(
        z_hi.reshape(1),
        space_in,
        keep.reshape(8, 2, 64, 128),
        got.reshape(8, 2, 64, 128),
        outs[0],
    )
    space_grads, parts = lax.optimization_barrier((space_grads, parts))

    space_out = exchange(space_grads, "space")
    time_grads = time_attention(
        z_lo.reshape(1), time_in, [p.reshape(4, 2, 64, 128) for p in parts]
    )
    space_out, time_grads = lax.optimization_barrier((space_out, time_grads))
    time_out = exchange(time_grads, "tm")
    return unpack(space_out) + unpack(time_out)


def solution(mesh):
    tokens = P(None, "tm", "space", None)
    in_specs = (tokens,) * 8 + (P("space", None), P("tm", None))
    return jax.shard_map(
        on_device, mesh=mesh, in_specs=in_specs, out_specs=(tokens,) * 6, check_vma=False
    )
```

```python
import math

import jax
import jax.numpy as jnp
from jax import lax
from jax.experimental import pallas as pl
from jax.experimental.pallas import tpu as pltpu
from jax.sharding import PartitionSpec as P

HEAD_DIM = 128
SCALE = 1.0 / math.sqrt(HEAD_DIM)
LOG2E = math.log2(math.e)
VMEM = 48 * 1024 * 1024
BF16 = jnp.bfloat16
F32 = jnp.float32
WHOLE = pl.BlockSpec(memory_space=pltpu.VMEM)
SCALARS = pl.BlockSpec(memory_space=pltpu.SMEM)
LATER = pl.BlockSpec(memory_space=pl.ANY)
IN_HBM = pl.BlockSpec(memory_space=pltpu.HBM)


def permutation(move):
    pairs = []
    for s in range(16):
        for t in range(16):
            z, x, y, c = (s // 8) * 4 + t // 4, (s // 2) % 4, t % 4, s % 2
            z2, x2, y2, c2 = move(z, x, y, c)
            z2, x2, y2, c2 = z2 % 8, x2 % 4, y2 % 4, c2 % 2
            pairs.append((s * 16 + t, ((z2 // 4) * 8 + x2 * 2 + c2) * 16 + (z2 % 4) * 4 + y2))
    return pairs


def send(array, move):
    return lax.ppermute(array, ("space", "tm"), permutation(move))


def twin(array):
    return send(array, lambda z, x, y, c: (z, x, y, 1 - c))


def nt(a, b):
    return lax.dot_general(a, b, (((1,), (1,)), ((), ())), preferred_element_type=F32)


def nn(a, b):
    return lax.dot_general(a, b, (((1,), (0,)), ((), ())), preferred_element_type=F32)


def call(kernel, out_shape, flops, size, **kw):
    return pl.pallas_call(
        kernel,
        out_shape=out_shape,
        compiler_params=pltpu.CompilerParams(vmem_limit_bytes=VMEM),
        cost_estimate=pl.CostEstimate(flops=flops, bytes_accessed=size, transcendentals=0),
        **kw,
    )


def pack_kernel(a_ref, b_ref, c_ref, *refs):
    out_ref = refs[-1]
    for t, ref in enumerate((a_ref, b_ref, c_ref)):
        for h in range(16):
            out_ref[h, t] = ref[:, h * 128 : (h + 1) * 128]


def pack(a, b, c, *after):
    flat = [v.reshape(128, 2048) for v in (a, b, c)]
    out = call(
        pack_kernel,
        jax.ShapeDtypeStruct((16, 3, 128, 128), BF16),
        0,
        3 << 20,
        in_specs=[WHOLE] * (3 + len(after)),
    )(*flat, *after)
    return out.reshape(16, 3, 2, 64, 128)


def unpack_kernel(in_ref, a_ref, b_ref, c_ref):
    for t, ref in enumerate((a_ref, b_ref, c_ref)):
        for h in range(16):
            ref[:, h * 128 : (h + 1) * 128] = in_ref[h, t]


def unpack(array):
    shape = jax.ShapeDtypeStruct((128, 2048), BF16)
    outs = call(unpack_kernel, (shape,) * 3, 0, 3 << 20)(array.reshape(16, 3, 128, 128))
    return tuple(v.reshape(2, 1, 64, 2048) for v in outs)


def rows_kernel(at_ref, space_ref, time_ref, rows_ref, both_ref, sems):
    half = space_ref.at[pl.ds(pl.multiple_of(at_ref[0] * 64, 64), 64), :]
    rows = time_ref.at[pl.ds(pl.multiple_of(at_ref[1] * 64, 64), 64), :]
    quarter = time_ref.at[pl.ds(pl.multiple_of(at_ref[2] * 32, 32), 32), :]
    copies = [
        pltpu.make_async_copy(rows, rows_ref, sems.at[0]),
        pltpu.make_async_copy(half, both_ref.at[:64], sems.at[1]),
        pltpu.make_async_copy(quarter, both_ref.at[64:], sems.at[2]),
    ]
    for copy in copies:
        copy.start()
    for copy in copies:
        copy.wait()


def rows_to_send(at, proj_space, proj_time):
    return call(
        rows_kernel,
        (jax.ShapeDtypeStruct((64, 2048), BF16), jax.ShapeDtypeStruct((96, 2048), BF16)),
        0,
        1 << 20,
        in_specs=[SCALARS] + [IN_HBM] * 2,
        out_specs=(WHOLE, WHOLE),
        scratch_shapes=[pltpu.SemaphoreType.DMA((3,))],
    )(at, proj_space, proj_time)


def gathered_kernel(both_ref, rows_ref, half_ref, along_z_ref):
    half_ref[...] = both_ref[:64]
    along_z_ref[:64] = rows_ref[...]
    along_z_ref[64:] = both_ref[64:]


def gathered(both, rows):
    return call(
        gathered_kernel,
        (jax.ShapeDtypeStruct((64, 2048), BF16), jax.ShapeDtypeStruct((96, 2048), BF16)),
        0,
        1 << 20,
        in_specs=[WHOLE] * 2,
    )(both, rows)


def pair_kernel(a_ref, b_ref, *refs):
    out_ref = refs[-1]
    out_ref[0] = a_ref[...]
    out_ref[1] = b_ref[...]


def pair(a, b, *after):
    shape = jax.ShapeDtypeStruct((2, 96, 2048), BF16)
    return call(pair_kernel, shape, 0, 1 << 20, in_specs=[WHOLE] * (2 + len(after)))(a, b, *after)


def stack_kernel(a_ref, b_ref, c_ref, d_ref, out_ref):
    for i, ref in enumerate((a_ref, b_ref, c_ref, d_ref)):
        out_ref[i] = ref[...]


def stacked(shards):
    shape = jax.ShapeDtypeStruct((4, 128, 2048), BF16)
    return call(stack_kernel, shape, 0, 4 << 20, in_specs=[WHOLE] * 4)(*shards)


def space_proj_kernel(at_ref, *refs):
    own_ref, twin_ref, w_own, w_half, w_rest = refs[:5]
    keep, other, weight_ref = refs[-3:]
    weight_ref[:128] = w_own[...]
    first = 128 + at_ref[1] * 64
    rest = 128 + (1 - at_ref[1]) * 64
    weight_ref[pl.ds(pl.multiple_of(first, 64), 64)] = w_half[...]
    weight_ref[pl.ds(pl.multiple_of(rest, 64), 64)] = w_rest[...]
    for i in range(8):
        at = at_ref[0] ^ i
        out = nt((own_ref, twin_ref)[i % 2][i // 2], weight_ref[...]).astype(BF16)
        keep[at] = out[:, :128]
        other[at] = out[:, 128:]


def space_proj(at, own, twins, w_own, w_half, w_rest, *after):
    shape = jax.ShapeDtypeStruct((8, 128, 128), BF16)
    return call(
        space_proj_kernel,
        (shape, shape),
        1 << 30,
        6 << 20,
        in_specs=[SCALARS] + [WHOLE] * (5 + len(after)),
        scratch_shapes=[pltpu.VMEM((256, 2048), BF16)],
    )(at, own, twins, w_own, w_half, w_rest, *after)


def time_proj_kernel(at_ref, *refs):
    shards, own, pieces, outs, weight_ref = refs[:4], refs[4], refs[5:7], refs[7:11], refs[11]
    weight_ref[:128] = own[...]
    for i in range(4):
        quarter = at_ref[1] ^ i
        core, half = quarter & 1, quarter >> 1
        row = 128 * (3 - 2 * core) + 64 * half
        weight_ref[pl.ds(pl.multiple_of(row, 64), 64)] = pieces[i % 2][i // 2, :64]
        row = 256 + 32 * quarter
        weight_ref[pl.ds(pl.multiple_of(row, 32), 32)] = pieces[i % 2][i // 2, 64:]
    for i in range(4):
        out = nt(shards[i][...], weight_ref[...]).astype(BF16)
        for k in range(4):
            outs[k][at_ref[0] ^ i] = out[:, k * 128 : (k + 1) * 128]


def time_proj(at, shards, own, rows, twin_rows):
    shape = jax.ShapeDtypeStruct((4, 128, 128), BF16)
    return call(
        time_proj_kernel,
        (shape,) * 4,
        1 << 30,
        5 << 20,
        in_specs=[SCALARS] + [WHOLE] * 7,
        scratch_shapes=[pltpu.VMEM((512, 2048), BF16)],
    )(at, *shards, own, rows, twin_rows)


def attend(q, k, v, o, k_t, mask):
    s = nt(k, q)
    if mask is not None:
        s = jnp.where(mask, s, -1e30)
    e = jnp.exp2((s - jnp.max(s, axis=0, keepdims=True)) * (SCALE * LOG2E))
    p = e * (1.0 / jnp.sum(e, axis=0, keepdims=True))
    dv = nn(p.astype(BF16), o)
    dp = nt(v, o)
    delta = jnp.sum(p * dp, axis=0, keepdims=True)
    ds = (p * (dp - delta)).astype(BF16)
    dk = nn(ds, q)
    dq_t = nn(k_t, ds)
    return dq_t, dk, dv


def space_kernel(pos_ref, qkv_ref, keep_ref, got_ref, after_ref, out_ref, o_ref):
    z_hi = pos_ref[0]
    o_ref[pl.ds(pl.multiple_of(z_hi * 512, 512), 512), :] = keep_ref[...].reshape(512, 128)
    o_ref[pl.ds(pl.multiple_of((1 - z_hi) * 512, 512), 512), :] = got_ref[...].reshape(512, 128)
    q, k, v = (qkv_ref[:, t].reshape(1024, 128) for t in range(3))
    dq_t, dk, dv = attend(q, k, v, o_ref[...], k.T, None)
    out_ref[:, 0] = (dq_t * SCALE).T.astype(BF16).reshape(16, 1, 64, 128)
    out_ref[:, 1] = (dk * SCALE).astype(BF16).reshape(16, 1, 64, 128)
    out_ref[:, 2] = dv.astype(BF16).reshape(16, 1, 64, 128)


def space_attention(z_hi, qkv, keep, got, after):
    whole = pl.BlockSpec((16, 3, 1, 64, 128), lambda b: (0, 0, b, 0, 0))
    half = pl.BlockSpec((8, 1, 64, 128), lambda b: (0, b, 0, 0))
    return call(
        space_kernel,
        jax.ShapeDtypeStruct((16, 3, 2, 64, 128), BF16),
        5 * (1 << 29),
        4 << 20,
        grid=(2,),
        in_specs=[SCALARS, whole, half, half, LATER],
        out_specs=whole,
        scratch_shapes=[pltpu.VMEM((1024, 128), BF16)],
    )(z_hi, qkv, keep, got, after)


def time_kernel(pos_ref, qkv_ref, *refs):
    parts, out_ref, o_ref = refs[:4], refs[4], refs[5]
    for i in range(4):
        o_ref[pl.ds(((pos_ref[0] - i) & 3) * 4, 4)] = parts[i][:, 0]
    rows = lax.broadcasted_iota(jnp.int32, (256, 256), 0)
    columns = lax.broadcasted_iota(jnp.int32, (256, 256), 1)
    mask = ((rows ^ columns) & 15) == 0
    for i in range(4):
        at = slice(16 * i, 16 * (i + 1))
        q = qkv_ref[:, 0, 0, at].reshape(256, 128)
        k = qkv_ref[:, 1, 0, at].reshape(256, 128)
        v = qkv_ref[:, 2, 0, at].reshape(256, 128)
        o = o_ref[:, at].reshape(256, 128)
        dq_t, dk, dv = attend(q, k, v, o, k.T, mask)
        out_ref[:, 0, 0, at] = (dq_t * SCALE).T.astype(BF16).reshape(16, 16, 128)
        out_ref[:, 1, 0, at] = (dk * SCALE).astype(BF16).reshape(16, 16, 128)
        out_ref[:, 2, 0, at] = dv.astype(BF16).reshape(16, 16, 128)


def time_attention(z_lo, qkv, parts):
    whole = pl.BlockSpec((16, 3, 1, 64, 128), lambda b: (0, 0, b, 0, 0))
    quarter = pl.BlockSpec((4, 1, 64, 128), lambda b: (0, b, 0, 0))
    return call(
        time_kernel,
        jax.ShapeDtypeStruct((16, 3, 2, 64, 128), BF16),
        5 * (1 << 27),
        4 << 20,
        grid=(2,),
        in_specs=[SCALARS, whole] + [quarter] * 4,
        out_specs=whole,
        scratch_shapes=[pltpu.VMEM((16, 64, 128), BF16)],
    )(z_lo, qkv, *parts)


def exchange(array, axis):
    return lax.all_to_all(array, axis, split_axis=0, concat_axis=0, tiled=True)


def on_device(
    query_space,
    key_space,
    value_space,
    query_time,
    key_time,
    value_time,
    block_grad,
    branch_grad,
    proj_space,
    proj_time,
):
    place_s, place_t = lax.axis_index("space"), lax.axis_index("tm")
    z_hi, xc = place_s // 8, place_s % 8
    z_lo, y = place_t // 4, place_t % 4

    time_in = exchange(pack(query_time, key_time, value_time), "tm")
    grad = block_grad.reshape(128, 2048)
    along_x = stacked(
        [grad] + [send(grad, lambda z, x, y, c, k=k: (z, x ^ k, y, c)) for k in (1, 2, 3)]
    )
    half = xc // 2 % 2
    rows, both = rows_to_send(jnp.stack([y % 2, half, xc % 4]), proj_space, proj_time)
    both = send(both, lambda z, x, y, c: (z + (-2 if z % 4 < 2 else 2), x, y, c))
    rows = send(rows, lambda z, x, y, c: (z + 1 - 2 * c, x, y, c))
    w_half, along_z = gathered(both, rows)
    cotangent = (block_grad.astype(F32) + branch_grad.astype(F32)).astype(BF16).reshape(128, 2048)
    along_y = [cotangent] + [
        send(cotangent, lambda z, x, y, c, k=k: (z, x, y ^ k, c)) for k in (1, 2, 3)
    ]

    space_packed = pack(
        query_space, key_space, value_space, along_x, w_half, along_z, along_y[1]
    )
    space_packed, time_in = lax.optimization_barrier((space_packed, time_in))
    space_in = exchange(space_packed, "space")
    w_rest = send(w_half, lambda z, x, y, c: (z, x, y ^ 1, c))
    along_z2 = send(along_z, lambda z, x, y, c: (z, x ^ 1, y, c))
    keep, other = space_proj(
        jnp.stack([xc, y % 2]),
        along_x,
        twin(along_x),
        proj_space,
        w_half,
        w_rest,
        along_y[2],
    )
    got = send(other, lambda z, x, y, c: (z + 4, x, y, c))
    pieces = pair(along_z, along_z2, keep, along_y[3])
    outs = time_proj(jnp.stack([y, xc % 4]), along_y, proj_time, pieces, twin(pieces))

    parts = [outs[0]] + [
        lax.ppermute(outs[k], "tm", [(t, (t // 4 + k) % 4 * 4 + t % 4) for t in range(16)])
        for k in (1, 2, 3)
    ]
    space_grads = space_attention(
        z_hi.reshape(1),
        space_in,
        keep.reshape(8, 2, 64, 128),
        got.reshape(8, 2, 64, 128),
        outs[0],
    )
    space_grads, parts = lax.optimization_barrier((space_grads, parts))

    space_out = exchange(space_grads, "space")
    time_grads = time_attention(
        z_lo.reshape(1), time_in, [p.reshape(4, 2, 64, 128) for p in parts]
    )
    space_out, time_grads = lax.optimization_barrier((space_out, time_grads))
    time_out = exchange(time_grads, "tm")
    return unpack(space_out) + unpack(time_out)


def solution(mesh):
    tokens = P(None, "tm", "space", None)
    in_specs = (tokens,) * 8 + (P("space", None), P("tm", None))
    return jax.shard_map(
        on_device, mesh=mesh, in_specs=in_specs, out_specs=(tokens,) * 6, check_vma=False
    )
```

```python
import math

import jax
import jax.numpy as jnp
from jax import lax
from jax.experimental import pallas as pl
from jax.experimental.pallas import tpu as pltpu
from jax.sharding import PartitionSpec as P

HEAD_DIM = 128
SCALE = 1.0 / math.sqrt(HEAD_DIM)
LOG2E = math.log2(math.e)
VMEM = 48 * 1024 * 1024
BF16 = jnp.bfloat16
F32 = jnp.float32
WHOLE = pl.BlockSpec(memory_space=pltpu.VMEM)
SCALARS = pl.BlockSpec(memory_space=pltpu.SMEM)
LATER = pl.BlockSpec(memory_space=pl.ANY)
IN_HBM = pl.BlockSpec(memory_space=pltpu.HBM)


def permutation(move):
    pairs = []
    for s in range(16):
        for t in range(16):
            z, x, y, c = (s // 8) * 4 + t // 4, (s // 2) % 4, t % 4, s % 2
            z2, x2, y2, c2 = move(z, x, y, c)
            z2, x2, y2, c2 = z2 % 8, x2 % 4, y2 % 4, c2 % 2
            pairs.append((s * 16 + t, ((z2 // 4) * 8 + x2 * 2 + c2) * 16 + (z2 % 4) * 4 + y2))
    return pairs


def send(array, move):
    return lax.ppermute(array, ("space", "tm"), permutation(move))


def twin(array):
    return send(array, lambda z, x, y, c: (z, x, y, 1 - c))


def nt(a, b):
    return lax.dot_general(a, b, (((1,), (1,)), ((), ())), preferred_element_type=F32)


def nn(a, b):
    return lax.dot_general(a, b, (((1,), (0,)), ((), ())), preferred_element_type=F32)


def call(kernel, out_shape, flops, size, **kw):
    return pl.pallas_call(
        kernel,
        out_shape=out_shape,
        compiler_params=pltpu.CompilerParams(vmem_limit_bytes=VMEM),
        cost_estimate=pl.CostEstimate(flops=flops, bytes_accessed=size, transcendentals=0),
        **kw,
    )


def pack_kernel(a_ref, b_ref, c_ref, *refs):
    out_ref = refs[-1]
    for t, ref in enumerate((a_ref, b_ref, c_ref)):
        for h in range(16):
            out_ref[h, t] = ref[:, h * 128 : (h + 1) * 128]


def pack(a, b, c, *after):
    flat = [v.reshape(128, 2048) for v in (a, b, c)]
    out = call(
        pack_kernel,
        jax.ShapeDtypeStruct((16, 3, 128, 128), BF16),
        0,
        3 << 20,
        in_specs=[WHOLE] * (3 + len(after)),
    )(*flat, *after)
    return out.reshape(16, 3, 2, 64, 128)


def pack_now(a, b, c):
    flat = [v.reshape(128, 2048) for v in (a, b, c)]
    out = pl.pallas_call(
        pack_kernel,
        out_shape=jax.ShapeDtypeStruct((16, 3, 128, 128), BF16),
        grid=(4,),
        in_specs=[pl.BlockSpec((32, 2048), lambda i: (i, 0))] * 3,
        out_specs=pl.BlockSpec((16, 3, 32, 128), lambda i: (0, 0, i, 0)),
        compiler_params=pltpu.CompilerParams(vmem_limit_bytes=62 * 1024 * 1024),
        cost_estimate=pl.CostEstimate(flops=0, bytes_accessed=3 << 20, transcendentals=0),
    )(*flat)
    return out.reshape(16, 3, 2, 64, 128)


def unpack_kernel(in_ref, a_ref, b_ref, c_ref):
    for t, ref in enumerate((a_ref, b_ref, c_ref)):
        for h in range(16):
            ref[:, h * 128 : (h + 1) * 128] = in_ref[h, t]


def unpack(array):
    shape = jax.ShapeDtypeStruct((128, 2048), BF16)
    outs = call(unpack_kernel, (shape,) * 3, 0, 3 << 20)(array.reshape(16, 3, 128, 128))
    return tuple(v.reshape(2, 1, 64, 2048) for v in outs)


def rows_kernel(at_ref, space_ref, time_ref, rows_ref, both_ref, sems):
    half = space_ref.at[pl.ds(pl.multiple_of(at_ref[0] * 64, 64), 64), :]
    rows = time_ref.at[pl.ds(pl.multiple_of(at_ref[1] * 64, 64), 64), :]
    quarter = time_ref.at[pl.ds(pl.multiple_of(at_ref[2] * 32, 32), 32), :]
    copies = [
        pltpu.make_async_copy(rows, rows_ref, sems.at[0]),
        pltpu.make_async_copy(half, both_ref.at[:64], sems.at[1]),
        pltpu.make_async_copy(quarter, both_ref.at[64:], sems.at[2]),
    ]
    for copy in copies:
        copy.start()
    for copy in copies:
        copy.wait()


def rows_to_send(at, proj_space, proj_time):
    return call(
        rows_kernel,
        (jax.ShapeDtypeStruct((64, 2048), BF16), jax.ShapeDtypeStruct((96, 2048), BF16)),
        0,
        1 << 20,
        in_specs=[SCALARS] + [IN_HBM] * 2,
        out_specs=(WHOLE, WHOLE),
        scratch_shapes=[pltpu.SemaphoreType.DMA((3,))],
    )(at, proj_space, proj_time)


def gathered_kernel(both_ref, rows_ref, half_ref, along_z_ref):
    half_ref[...] = both_ref[:64]
    along_z_ref[:64] = rows_ref[...]
    along_z_ref[64:] = both_ref[64:]


def gathered(both, rows):
    return call(
        gathered_kernel,
        (jax.ShapeDtypeStruct((64, 2048), BF16), jax.ShapeDtypeStruct((96, 2048), BF16)),
        0,
        1 << 20,
        in_specs=[WHOLE] * 2,
    )(both, rows)


def ready_kernel(a_ref, *refs):
    refs[-1][...] = a_ref[:16, :128]


def ready(*arrays):
    shape = jax.ShapeDtypeStruct((16, 128), BF16)
    return call(ready_kernel, shape, 0, 1 << 12, in_specs=[WHOLE] * len(arrays))(*arrays)


def pair_kernel(a_ref, b_ref, *refs):
    out_ref = refs[-1]
    out_ref[0] = a_ref[...]
    out_ref[1] = b_ref[...]


def pair(a, b, *after):
    shape = jax.ShapeDtypeStruct((2, 96, 2048), BF16)
    return call(pair_kernel, shape, 0, 1 << 20, in_specs=[WHOLE] * (2 + len(after)))(a, b, *after)


def stack_kernel(a_ref, b_ref, c_ref, d_ref, out_ref):
    for i, ref in enumerate((a_ref, b_ref, c_ref, d_ref)):
        out_ref[i] = ref[...]


def stacked(shards):
    shape = jax.ShapeDtypeStruct((4, 128, 2048), BF16)
    return call(stack_kernel, shape, 0, 4 << 20, in_specs=[WHOLE] * 4)(*shards)


def space_proj_kernel(at_ref, *refs):
    own_ref, twin_ref, w_own, w_half, w_rest = refs[:5]
    keep, other, weight_ref = refs[-3:]
    weight_ref[:128] = w_own[...]
    first = 128 + at_ref[1] * 64
    rest = 128 + (1 - at_ref[1]) * 64
    weight_ref[pl.ds(pl.multiple_of(first, 64), 64)] = w_half[...]
    weight_ref[pl.ds(pl.multiple_of(rest, 64), 64)] = w_rest[...]
    for i in range(8):
        at = at_ref[0] ^ i
        out = nt((own_ref, twin_ref)[i % 2][i // 2], weight_ref[...]).astype(BF16)
        keep[at] = out[:, :128]
        other[at] = out[:, 128:]


def space_proj(at, own, twins, w_own, w_half, w_rest, *after):
    shape = jax.ShapeDtypeStruct((8, 128, 128), BF16)
    return call(
        space_proj_kernel,
        (shape, shape),
        1 << 30,
        6 << 20,
        in_specs=[SCALARS] + [WHOLE] * (5 + len(after)),
        scratch_shapes=[pltpu.VMEM((256, 2048), BF16)],
    )(at, own, twins, w_own, w_half, w_rest, *after)


def time_proj_kernel(at_ref, *refs):
    shards, own, pieces, outs, weight_ref = refs[:4], refs[4], refs[5:7], refs[7:11], refs[11]
    weight_ref[:128] = own[...]
    for i in range(4):
        quarter = at_ref[1] ^ i
        core, half = quarter & 1, quarter >> 1
        row = 128 * (3 - 2 * core) + 64 * half
        weight_ref[pl.ds(pl.multiple_of(row, 64), 64)] = pieces[i % 2][i // 2, :64]
        row = 256 + 32 * quarter
        weight_ref[pl.ds(pl.multiple_of(row, 32), 32)] = pieces[i % 2][i // 2, 64:]
    for i in range(4):
        out = nt(shards[i][...], weight_ref[...]).astype(BF16)
        for k in range(4):
            outs[k][at_ref[0] ^ i] = out[:, k * 128 : (k + 1) * 128]


def time_proj(at, shards, own, rows, twin_rows):
    shape = jax.ShapeDtypeStruct((4, 128, 128), BF16)
    return call(
        time_proj_kernel,
        (shape,) * 4,
        1 << 30,
        5 << 20,
        in_specs=[SCALARS] + [WHOLE] * 7,
        scratch_shapes=[pltpu.VMEM((512, 2048), BF16)],
    )(at, *shards, own, rows, twin_rows)


def attend(q, k, v, o, k_t, mask):
    s = nt(k, q)
    if mask is not None:
        s = jnp.where(mask, s, -1e30)
    e = jnp.exp2((s - jnp.max(s, axis=0, keepdims=True)) * (SCALE * LOG2E))
    p = e * (1.0 / jnp.sum(e, axis=0, keepdims=True))
    dv = nn(p.astype(BF16), o)
    dp = nt(v, o)
    delta = jnp.sum(p * dp, axis=0, keepdims=True)
    ds = (p * (dp - delta)).astype(BF16)
    dk = nn(ds, q)
    dq_t = nn(k_t, ds)
    return dq_t, dk, dv


def space_kernel(pos_ref, qkv_ref, keep_ref, got_ref, after_ref, out_ref, o_ref):
    z_hi = pos_ref[0]
    o_ref[pl.ds(pl.multiple_of(z_hi * 512, 512), 512), :] = keep_ref[...].reshape(512, 128)
    o_ref[pl.ds(pl.multiple_of((1 - z_hi) * 512, 512), 512), :] = got_ref[...].reshape(512, 128)
    q, k, v = (qkv_ref[:, t].reshape(1024, 128) for t in range(3))
    dq_t, dk, dv = attend(q, k, v, o_ref[...], k.T, None)
    out_ref[:, 0] = (dq_t * SCALE).T.astype(BF16).reshape(16, 1, 64, 128)
    out_ref[:, 1] = (dk * SCALE).astype(BF16).reshape(16, 1, 64, 128)
    out_ref[:, 2] = dv.astype(BF16).reshape(16, 1, 64, 128)


def space_attention(z_hi, qkv, keep, got, after):
    whole = pl.BlockSpec((16, 3, 1, 64, 128), lambda b: (0, 0, b, 0, 0))
    half = pl.BlockSpec((8, 1, 64, 128), lambda b: (0, b, 0, 0))
    return call(
        space_kernel,
        jax.ShapeDtypeStruct((16, 3, 2, 64, 128), BF16),
        5 * (1 << 29),
        4 << 20,
        grid=(2,),
        in_specs=[SCALARS, whole, half, half, LATER],
        out_specs=whole,
        scratch_shapes=[pltpu.VMEM((1024, 128), BF16)],
    )(z_hi, qkv, keep, got, after)


def time_kernel(pos_ref, qkv_ref, *refs):
    parts, out_ref, o_ref = refs[:4], refs[4], refs[5]
    for i in range(4):
        o_ref[pl.ds(((pos_ref[0] - i) & 3) * 4, 4)] = parts[i][:, 0]
    rows = lax.broadcasted_iota(jnp.int32, (256, 256), 0)
    columns = lax.broadcasted_iota(jnp.int32, (256, 256), 1)
    mask = ((rows ^ columns) & 15) == 0
    for i in range(4):
        at = slice(16 * i, 16 * (i + 1))
        q = qkv_ref[:, 0, 0, at].reshape(256, 128)
        k = qkv_ref[:, 1, 0, at].reshape(256, 128)
        v = qkv_ref[:, 2, 0, at].reshape(256, 128)
        o = o_ref[:, at].reshape(256, 128)
        dq_t, dk, dv = attend(q, k, v, o, k.T, mask)
        out_ref[:, 0, 0, at] = (dq_t * SCALE).T.astype(BF16).reshape(16, 16, 128)
        out_ref[:, 1, 0, at] = (dk * SCALE).astype(BF16).reshape(16, 16, 128)
        out_ref[:, 2, 0, at] = dv.astype(BF16).reshape(16, 16, 128)


def time_attention(z_lo, qkv, parts):
    whole = pl.BlockSpec((16, 3, 1, 64, 128), lambda b: (0, 0, b, 0, 0))
    quarter = pl.BlockSpec((4, 1, 64, 128), lambda b: (0, b, 0, 0))
    return call(
        time_kernel,
        jax.ShapeDtypeStruct((16, 3, 2, 64, 128), BF16),
        5 * (1 << 27),
        4 << 20,
        grid=(2,),
        in_specs=[SCALARS, whole] + [quarter] * 4,
        out_specs=whole,
        scratch_shapes=[pltpu.VMEM((16, 64, 128), BF16)],
    )(z_lo, qkv, *parts)


def exchange(array, axis):
    return lax.all_to_all(array, axis, split_axis=0, concat_axis=0, tiled=True)


def on_device(
    query_space,
    key_space,
    value_space,
    query_time,
    key_time,
    value_time,
    block_grad,
    branch_grad,
    proj_space,
    proj_time,
):
    place_s, place_t = lax.axis_index("space"), lax.axis_index("tm")
    z_hi, xc = place_s // 8, place_s % 8
    z_lo, y = place_t // 4, place_t % 4

    time_in = exchange(pack_now(query_time, key_time, value_time), "tm")
    grad = block_grad.reshape(128, 2048)
    along_x = stacked(
        [grad] + [send(grad, lambda z, x, y, c, k=k: (z, x ^ k, y, c)) for k in (1, 2, 3)]
    )
    half = xc // 2 % 2
    rows, both = rows_to_send(jnp.stack([y % 2, half, xc % 4]), proj_space, proj_time)
    both = send(both, lambda z, x, y, c: (z + (-2 if z % 4 < 2 else 2), x, y, c))
    rows = send(rows, lambda z, x, y, c: (z + 1 - 2 * c, x, y, c))
    w_half, along_z = gathered(both, rows)
    cotangent = (block_grad.astype(F32) + branch_grad.astype(F32)).astype(BF16).reshape(128, 2048)
    along_y = [cotangent] + [
        send(cotangent, lambda z, x, y, c, k=k: (z, x, y ^ k, c)) for k in (1, 2, 3)
    ]

    space_packed = pack(query_space, key_space, value_space)
    first = ready(w_half, along_x, along_z, along_y[1])
    space_packed, time_in, first = lax.optimization_barrier((space_packed, time_in, first))
    space_in = exchange(space_packed, "space")
    w_rest = send(w_half, lambda z, x, y, c: (z, x, y ^ 1, c))
    along_z2 = send(along_z, lambda z, x, y, c: (z, x ^ 1, y, c))
    keep, other = space_proj(
        jnp.stack([xc, y % 2]),
        along_x,
        twin(along_x),
        proj_space,
        w_half,
        w_rest,
        along_y[2],
        first,
    )
    got = send(other, lambda z, x, y, c: (z + 4, x, y, c))
    pieces = pair(along_z, along_z2, keep, along_y[3])
    outs = time_proj(jnp.stack([y, xc % 4]), along_y, proj_time, pieces, twin(pieces))

    parts = [outs[0]] + [
        lax.ppermute(outs[k], "tm", [(t, (t // 4 + k) % 4 * 4 + t % 4) for t in range(16)])
        for k in (1, 2, 3)
    ]
    space_grads = space_attention(
        z_hi.reshape(1),
        space_in,
        keep.reshape(8, 2, 64, 128),
        got.reshape(8, 2, 64, 128),
        outs[0],
    )
    space_grads, parts = lax.optimization_barrier((space_grads, parts))

    space_out = exchange(space_grads, "space")
    time_grads = time_attention(
        z_lo.reshape(1), time_in, [p.reshape(4, 2, 64, 128) for p in parts]
    )
    space_out, time_grads = lax.optimization_barrier((space_out, time_grads))
    time_out = exchange(time_grads, "tm")
    return unpack(space_out) + unpack(time_out)


def solution(mesh):
    tokens = P(None, "tm", "space", None)
    in_specs = (tokens,) * 8 + (P("space", None), P("tm", None))
    return jax.shard_map(
        on_device, mesh=mesh, in_specs=in_specs, out_specs=(tokens,) * 6, check_vma=False
    )
```
